256 devices in a mesh: phase: 8 (over x, core), seq: 16 (over y_lo, z), mp: 2 (over y_hi).
Axes of the slice: x: 4, y: 4 (y_hi: 2, y_lo: 2; y = y_hi * 2 + y_lo), z: 8, core: 2. Of those that a mesh axis runs over, the one named last changes fastest.
Arguments:
- queries: bfloat16 [8, 8192, 4096], P('phase', 'seq', 'mp'), may hold values from -360 to 360
- key_weight: bfloat16 [8, 1024, 4096], P('phase', None, 'mp'), may hold values from -0.1875 to 0.1875
- value_weight: bfloat16 [8, 1024, 4096], P('phase', None, 'mp'), may hold values from -0.1875 to 0.1875
- enc_gain: float32 [1024], replicated, may hold values from 0.25 to 2
- neighbour_states: bfloat16 [512, 64, 1024], P('seq', ('phase', 'mp')), may hold values from -600 to 600
- slot_dest: int32 [512], P('seq'), may hold values from -1 to 255, as said below
Outputs:
- context: bfloat16 [8, 8192, 4096], P('phase', 'seq', 'mp')
The draws below stay inside these ranges and needn't reach their ends.
Inputs may be any that keep to these rules, and one draw needn't show every extreme that they name: slot_dest names every position 0 to 255 exactly once and is -1 elsewhere. Positions 2 * 8 j to 2 * 8 (j + 1) - 1 belong to the tokens of index j of seq. The slots of one index of seq name at most 2 positions of any one index of seq, and this bound is reached; one index of seq has up to 32 filled slots, reached in every draw.
All inputs are finite; a program needn't handle non-finite values.
Results may differ from the reference program's by a relative error of at most 0.0074.
Values may be sent and summed in bfloat16 or wider, within the bound.
A program may use at most 64 MiB of HBM per device.

```python
import math
import jax
import jax.numpy as jnp
from jax import lax

DE = 1024
HEADS = 32
HD = 128
SEGLEN = 64
NLEN = 64
NEIGH = 2
HQ = 4096
CH_DEV = 8
PHASES = 8
SHARDS = 16
TOKENS = 8192
SEQLEN = 8192
NB_DEV = 32
SLOTS = 512


def draw_queries(key, part):
    base = jnp.clip(jax.random.normal(key, (PHASES, TOKENS, HQ), jnp.float32), -6.0, 6.0)
    return base.astype(jnp.bfloat16)


def draw_neighbour_states(key, part):
    keys = jax.random.split(jax.random.fold_in(key, 11), 3)
    base = jnp.clip(jax.random.normal(keys[0], (SLOTS, NLEN, DE), jnp.float32), -6.0, 6.0)
    column = jnp.exp(jax.random.uniform(keys[1], (DE,), jnp.float32, 0.0, math.log(10.0)))
    rowscale = jnp.exp(jax.random.uniform(keys[2], (SLOTS, NLEN, 1), jnp.float32, 0.0, math.log(10.0)))
    return (base * column * rowscale).astype(jnp.bfloat16)


def draw_slot_dest(key, part):
    count = SHARDS
    per_shard = NEIGH * CH_DEV
    slots_here = NB_DEV
    baseline = per_shard // count
    keys = jax.random.split(jax.random.fold_in(key, 23), 5)
    order = jax.random.permutation(keys[0], count)
    takers = order[0::2]
    givers = order[1::2]
    amount = jax.random.randint(keys[1], (count // 2,), 0, count + 1).at[0].set(count)
    column_perm = jax.vmap(lambda single: jax.random.permutation(single, count))(jax.random.split(keys[2], count // 2))
    column_rank = jnp.argsort(column_perm, axis=1)
    moved = (column_rank < amount[:, None]).astype(jnp.int32)
    senders = jnp.arange(count)
    taker_hot = (takers[:, None] == senders[None, :]).astype(jnp.int32)
    giver_hot = (givers[:, None] == senders[None, :]).astype(jnp.int32)
    counts = baseline + jnp.dot(taker_hot.T, moved) - jnp.dot(giver_hot.T, moved)
    filled = jnp.sum(counts, axis=1)
    running = jnp.cumsum(counts, axis=1)
    slot_index = jnp.arange(slots_here)
    receiver = jnp.sum((running[:, None, :] <= slot_index[None, :, None]).astype(jnp.int32), axis=2)
    is_live = slot_index[None, :] < filled[:, None]
    receiver = jnp.minimum(receiver, count - 1)
    pair_start = jnp.take_along_axis(running - counts, receiver, axis=1)
    slot_rank = slot_index[None, :] - pair_start
    column_start = jnp.cumsum(counts, axis=0) - counts
    first_place = jnp.take_along_axis(column_start, receiver, axis=1) + slot_rank
    receiver_perm = jax.vmap(lambda single: jax.random.permutation(single, per_shard))(jax.random.split(keys[3], count))
    place = receiver_perm[receiver, jnp.clip(first_place, 0, per_shard - 1)]
    dest = jnp.where(is_live, receiver * per_shard + place, -1)
    slot_perm = jax.vmap(lambda single: jax.random.permutation(single, slots_here))(jax.random.split(keys[4], count))
    dest = jnp.take_along_axis(dest, slot_perm, axis=1)
    return dest.reshape(count * slots_here).astype(jnp.int32)


def level_of(stream_key, dims, shards, smallest, top_value):
    gain, own = 1.0, jax.random.fold_in(stream_key, 6)
    for dim, parts in shards:
        draws = jnp.exp(jax.random.uniform(jax.random.fold_in(own, dim), (parts,), jnp.float32, smallest / len(shards), top_value / len(shards)))
        gain = gain * jnp.repeat(draws, dims[dim] // parts).reshape([-1 if axis == dim else 1 for axis in range(len(dims))])
    return gain


def normal_values(stream_key, dims, deviation, bound, pieces=(), dtype=jnp.bfloat16):
    values = jax.random.normal(stream_key, dims, jnp.float32) * deviation
    if len(pieces) > 0:
        values = level_of(stream_key, dims, pieces, -0.22, 0.18) * values
    return jnp.clip(values, min=-bound, max=bound).astype(dtype)


def setup_inputs(seed: int = 0) -> dict:
    splits = jax.random.split(jax.random.key(seed), 7)
    return {
        "queries": draw_queries(jax.random.fold_in(splits[6], 71), 0),
        "key_weight": normal_values(splits[1], (PHASES, DE, HQ), DE ** -0.5, 0.1875, ((0, 8), (2, 2))),
        "value_weight": normal_values(splits[2], (PHASES, DE, HQ), DE ** -0.5, 0.1875, ((0, 8), (2, 2))),
        "enc_gain": jnp.clip(jax.random.uniform(splits[3], (DE,), jnp.float32, 0.25, 2.0), 0.25, 2.0),
        "neighbour_states": draw_neighbour_states(jax.random.fold_in(splits[6], 71), 0),
        "slot_dest": draw_slot_dest(jax.random.fold_in(splits[6], 71), 0),
    }


def reference(queries, key_weight, value_weight, enc_gain, neighbour_states, slot_dest):
    positions = NEIGH * CH_DEV * SHARDS
    states = neighbour_states.astype(jnp.float32)
    meansq = lax.optimization_barrier(jnp.mean(states * states, axis=-1, keepdims=True))
    normed = (states * lax.rsqrt(meansq + 1e-06) * enc_gain.astype(jnp.float32)).astype(jnp.bfloat16)
    target = jnp.where(slot_dest >= 0, slot_dest, positions).astype(jnp.int32)
    neighbours = jnp.zeros((positions + 1, NLEN, DE), jnp.bfloat16).at[target].set(normed)[:positions]
    sequences = TOKENS // SEQLEN
    per_seq = SEQLEN // SEGLEN
    flattened = neighbours.reshape(positions * NLEN, DE)

    def one_phase(operands):
        query_rows, key_mat, value_mat = operands
        keys = jnp.dot(flattened, key_mat, preferred_element_type=jnp.float32).astype(jnp.bfloat16)
        vals = jnp.dot(flattened, value_mat, preferred_element_type=jnp.float32).astype(jnp.bfloat16)
        keys = keys.reshape(sequences, per_seq, NEIGH * NLEN, HQ)
        vals = vals.reshape(sequences, per_seq, NEIGH * NLEN, HQ)
        empty_block = jnp.zeros((sequences, 1, NEIGH * NLEN, HQ), jnp.bfloat16)
        all_keys = jnp.concatenate([empty_block, keys], axis=1).reshape(sequences, per_seq + 1, NEIGH * NLEN, HEADS, HD)
        all_vals = jnp.concatenate([empty_block, vals], axis=1).reshape(sequences, per_seq + 1, NEIGH * NLEN, HEADS, HD)
        seq_rows = query_rows.reshape(sequences, SEQLEN, HQ)
        padded = jnp.concatenate([jnp.zeros((sequences, 1, HQ), jnp.bfloat16), seq_rows, jnp.zeros((sequences, SEGLEN - 1, HQ), jnp.bfloat16)], axis=1)
        padded = padded.reshape(sequences, per_seq + 1, SEGLEN, HEADS, HD)
        scores = jnp.einsum('swqhd,swkhd->swhqk', padded.astype(jnp.float32), all_keys.astype(jnp.float32), precision=lax.Precision.HIGHEST) * HD ** (-0.5)
        top = lax.optimization_barrier(jnp.max(scores, axis=-1, keepdims=True))
        exponent = jnp.exp(scores - top)
        weights = (exponent / lax.optimization_barrier(jnp.sum(exponent, axis=-1, keepdims=True))).astype(jnp.bfloat16)
        context = jnp.einsum('swhqk,swkhd->swqhd', weights.astype(jnp.float32), all_vals.astype(jnp.float32), precision=lax.Precision.HIGHEST)
        context = context.astype(jnp.bfloat16).reshape(sequences, (per_seq + 1) * SEGLEN, HQ)[:, 1:SEQLEN + 1]
        keep = jnp.arange(SEQLEN) >= SEGLEN - 1
        context = jnp.where(keep[None, :, None], context, jnp.zeros_like(context))
        return context.reshape(TOKENS, HQ)
    return lax.map(one_phase, (queries, key_weight, value_weight))
```

```python
import jax
import jax.numpy as jnp
from jax import lax
from jax.experimental import pallas as pl
from jax.experimental.pallas import tpu as pltpu
from jax.sharding import PartitionSpec as P

MESH = pl.DeviceIdType.MESH
BF = jnp.bfloat16
F32 = jnp.float32

HD = 128
SEGLEN = 64
SEQ = 16
CHIPS = 8
CHUNKS = 4
ORDER = (1, 0, 2, 3)
EXP2_SCALE = HD ** (-0.5) * 1.4426950408889634


def iota(shape, dim):
    return lax.broadcasted_iota(jnp.int32, shape, dim)


def pack_rows(states_ref, gain_ref, dest_ref, sbuf):
    states = states_ref[...].astype(F32)
    meansq = jnp.mean(states * states, axis=-1, keepdims=True)
    normed = states * lax.rsqrt(meansq + 1e-06) * gain_ref[...].reshape(1, 1, -1)
    dest = dest_ref[...]
    row = iota((128, 32), 0)
    hit = lax.shift_right_arithmetic(dest, 4) == row // 8
    before = (iota((32, 32), 0) < iota((32, 32), 1)).astype(BF)
    rank = jnp.dot(hit.astype(BF), before, preferred_element_type=F32)
    pick = hit & (rank == ((row // 4) % 2).astype(F32))
    place = jnp.sum(jnp.where(pick, (dest + 1).astype(F32), 0.0), axis=1, keepdims=True)
    packed = jnp.zeros((128, 1024), F32)
    for r in range(4):
        one = (pick & (row % 4 == r)).astype(BF)
        packed += jnp.dot(one, normed[:, r, :].astype(BF), preferred_element_type=F32)
    left = packed[:, :512].reshape(SEQ, 8, 512)
    right = packed[:, 512:].reshape(SEQ, 8, 512)
    place = jnp.broadcast_to(place, (128, 128)).reshape(SEQ, 8, 128)
    sbuf[:, :, 0:512] = jnp.concatenate([left, right], axis=1).astype(BF)
    sbuf[:, :, 512:640] = jnp.concatenate([place, place], axis=1).astype(BF)


def unpack_rows(rbuf, me, piece):
    got = rbuf[...].astype(F32)
    place = got[:, :8, 512:].reshape(128, 128)
    row, lane = iota((128, 128), 0), iota((128, 128), 1)
    want = SEQ * me + 2 * (lane // 8 - 1) + (lane // 4) % 2 + 1
    match = (place == want.astype(F32)) & (row % 4 == lane % 4) & (lane >= 8) & (lane < 72)
    match = match.astype(BF)
    for half in range(2):
        rows = got[:, 8 * half : 8 * half + 8, :512].reshape(128, 512).astype(BF)
        out = lax.dot_general(match, rows, (((0,), (0,)), ((), ())), preferred_element_type=F32)
        piece[:, 512 * half : 512 * half + 512] = out[:80].astype(BF)


def by_window(rows):
    four = rows.reshape(16, 2, 8, rows.shape[1])
    return [four[:, w].reshape(128, rows.shape[1]).astype(BF) for w in range(2)]


def attend(c, n, me, gath, wk, wv, qs, outs):
    cols = pl.ds(pl.multiple_of(n * 256, 256), 256)
    near = gath[c].reshape(256, 1024)
    key = jnp.concatenate(by_window(jnp.dot(near, wk[:, cols], preferred_element_type=F32)), axis=0)
    val = jnp.concatenate(by_window(jnp.dot(near, wv[:, cols], preferred_element_type=F32)), axis=0)
    last = iota((16, 256), 0) == 15
    zero = jnp.zeros((SEGLEN, HD), BF)
    left = []
    for w in range(2):
        at = SEGLEN * (2 * c + w)
        head = qs[at + 16 : at + 64, cols]
        tail = jnp.where(last, qs[at : at + 16, cols], qs[at + 64 : at + 80, cols])
        query = jnp.concatenate([head, tail], axis=0)
        left.append(jnp.concatenate([query[:, :HD], zero], axis=1))
        left.append(jnp.concatenate([zero, query[:, HD:]], axis=1))
    scores = lax.dot_general(
        jnp.concatenate(left, axis=0), key, (((1,), (1,)), ((), ())), preferred_element_type=F32
    )
    weights = []
    for w in range(2):
        own = scores[128 * w : 128 * w + 128, 128 * w : 128 * w + 128]
        top = jnp.max(own, axis=-1, keepdims=True)
        exponent = jnp.exp2((own - top) * EXP2_SCALE)
        total = jnp.sum(exponent, axis=-1, keepdims=True)
        own = (exponent * (1.0 / total)).astype(BF)
        pad = jnp.zeros((128, 128), BF)
        weights.append(jnp.concatenate([own, pad] if w == 0 else [pad, own], axis=1))
    context = jnp.dot(jnp.concatenate(weights, axis=0), val, preferred_element_type=F32)
    for w in range(2):
        at = SEGLEN * (2 * c + w)
        two = context[128 * w : 128 * w + 128]
        both = jnp.concatenate([two[:SEGLEN, :HD], two[SEGLEN:, HD:]], axis=1)
        if c == 0 and w == 0:
            keep = (iota((SEGLEN, 256), 0) == SEGLEN - 1) | (me > 0)
            both = jnp.where(keep, both, 0.0)
        both = both.astype(BF)
        outs[at + 16 : at + 64, cols] = both[:48]
        outs[at : at + 16, cols] = jnp.where(last, both[48:], outs[at : at + 16, cols])
        outs[at + 64 : at + 80, cols] = jnp.where(last, outs[at + 64 : at + 80, cols], both[48:])


def kernel(
    q_hbm, wk_hbm, wv_hbm, gain_ref, states_ref, dest_ref, out_hbm,
    sbuf, rbuf, piece, prev, gath, wk, wv, qs, outs, back,
    load_sem, route_send, route_recv, halo_send, halo_recv, gath_send, gath_recv, pair_send, pair_recv,
):
    phase, me, mp = lax.axis_index("phase"), lax.axis_index("seq"), lax.axis_index("mp")
    x, core = phase // 2, phase % 2
    chip = x * 2 + mp

    def at_seq(s):
        return (phase, s, mp)

    def at_chip(k):
        return ((k // 2) * 2 + core, me, k % 2)

    after, ahead = lax.rem(me + 1, SEQ), lax.rem(me + SEQ - 1, SEQ)
    partner = (x * 2 + 1 - core, me, mp)
    barrier = pltpu.get_barrier_semaphore()
    for off in range(1, SEQ):
        pl.semaphore_signal(barrier, inc=1, device_id=at_seq(lax.rem(me + off, SEQ)), device_id_type=MESH)
    for off in range(1, CHIPS):
        pl.semaphore_signal(barrier, inc=1, device_id=at_chip(lax.rem(chip + off, CHIPS)), device_id_type=MESH)
    pl.semaphore_signal(barrier, inc=1, device_id=partner, device_id_type=MESH)

    loads = [
        pltpu.make_async_copy(q_hbm.at[0], qs.at[pl.ds(16, 512)], load_sem.at[0]),
        pltpu.make_async_copy(wk_hbm.at[0], wk, load_sem.at[1]),
        pltpu.make_async_copy(wv_hbm.at[0], wv, load_sem.at[2]),
    ]
    for load in loads:
        load.start()
    pack_rows(states_ref, gain_ref, dest_ref, sbuf)
    outs[0:16] = jnp.zeros((16, 2048), BF)
    pl.semaphore_wait(barrier, SEQ - 1 + CHIPS - 1 + 1)

    def route(s, slot):
        return pltpu.make_async_remote_copy(
            src_ref=sbuf.at[s], dst_ref=rbuf.at[slot], send_sem=route_send.at[s], recv_sem=route_recv.at[slot],
            device_id=at_seq(s), device_id_type=MESH,
        )

    for off in range(1, SEQ):
        route(lax.rem(me + off, SEQ), me).start()
    query_halo = pltpu.make_async_remote_copy(
        src_ref=q_hbm.at[0, pl.ds(496, 16)], dst_ref=qs.at[pl.ds(0, 16)],
        send_sem=halo_send.at[0], recv_sem=halo_recv.at[0], device_id=at_seq(after), device_id_type=MESH,
    )
    query_halo.start()
    rbuf[me] = sbuf[me]
    for off in range(1, SEQ):
        s = lax.rem(me + SEQ - off, SEQ)
        route(s, s).wait_recv()
    unpack_rows(rbuf, me, piece)

    prev_halo = pltpu.make_async_remote_copy(
        src_ref=piece.at[pl.ds(64, 16)], dst_ref=prev,
        send_sem=halo_send.at[1], recv_sem=halo_recv.at[1], device_id=at_seq(after), device_id_type=MESH,
    )
    prev_halo.start()

    def give(c, k, slot):
        return pltpu.make_async_remote_copy(
            src_ref=gath.at[c, core, chip], dst_ref=gath.at[c, core, slot],
            send_sem=gath_send.at[c, k], recv_sem=gath_recv.at[c, slot],
            device_id=at_chip(k), device_id_type=MESH,
        )

    def across(c, side):
        return pltpu.make_async_remote_copy(
            src_ref=gath.at[c, core], dst_ref=gath.at[c, side], send_sem=pair_send.at[c], recv_sem=pair_recv.at[c],
            device_id=partner, device_id_type=MESH,
        )

    for c in ORDER:
        if c == 0:
            prev_halo.wait_recv()
            mine = jnp.where(iota((16, 1024), 0) < 8, prev[...], piece[0:16])
        else:
            mine = piece[16 * c : 16 * c + 16]
        gath[c, core, chip] = mine
        for off in range(1, CHIPS):
            give(c, lax.rem(chip + off, CHIPS), chip).start()

    def pass_on(c):
        for off in range(1, CHIPS):
            k = lax.rem(chip + CHIPS - off, CHIPS)
            give(c, k, k).wait_recv()
        across(c, core).start()

    ctx_halo = pltpu.make_async_remote_copy(
        src_ref=outs.at[pl.ds(0, 16)], dst_ref=back,
        send_sem=halo_send.at[2], recv_sem=halo_recv.at[2], device_id=at_seq(ahead), device_id_type=MESH,
    )
    pass_on(ORDER[0])
    for load in loads:
        load.wait()
    query_halo.wait_recv()
    for i, c in enumerate(ORDER):
        across(c, 1 - core).wait_recv()

        def step(n, carry, c=c):
            attend(c, n, me, gath, wk, wv, qs, outs)
            return carry

        lax.fori_loop(0, 4, step, 0)
        if i + 1 < CHUNKS:
            pass_on(ORDER[i + 1])
        lax.fori_loop(4, 8, step, 0)
        if c == 0:
            ctx_halo.start()

    ctx_halo.wait_recv()
    outs[512:528] = jnp.where(iota((16, 2048), 0) == 15, back[...], outs[512:528])
    store = pltpu.make_async_copy(outs.at[pl.ds(16, 512)], out_hbm.at[0], load_sem.at[3])
    store.start()
    for off in range(1, SEQ):
        route(lax.rem(me + off, SEQ), me).wait_send()
    query_halo.wait_send()
    prev_halo.wait_send()
    ctx_halo.wait_send()
    for c in ORDER:
        for off in range(1, CHIPS):
            give(c, lax.rem(chip + off, CHIPS), chip).wait_send()
        across(c, core).wait_send()
    store.wait()


def on_device(queries, key_weight, value_weight, enc_gain, neighbour_states, slot_dest):
    whole = pl.BlockSpec(memory_space=pltpu.VMEM)
    place = pl.BlockSpec(memory_space=pl.ANY)
    dma = pltpu.SemaphoreType.DMA
    return pl.pallas_call(
        kernel,
        out_shape=jax.ShapeDtypeStruct(queries.shape, BF),
        in_specs=[place, place, place, whole, whole, whole],
        out_specs=place,
        scratch_shapes=[
            pltpu.VMEM((SEQ, 16, 640), BF),
            pltpu.VMEM((SEQ, 16, 640), BF),
            pltpu.VMEM((80, 1024), BF),
            pltpu.VMEM((16, 1024), BF),
            pltpu.VMEM((CHUNKS, 2, CHIPS, 16, 1024), BF),
            pltpu.VMEM((1024, 2048), BF),
            pltpu.VMEM((1024, 2048), BF),
            pltpu.VMEM((528, 2048), BF),
            pltpu.VMEM((528, 2048), BF),
            pltpu.VMEM((16, 2048), BF),
            dma((4,)),
            dma((SEQ,)),
            dma((SEQ,)),
            dma((3,)),
            dma((3,)),
            dma((CHUNKS, CHIPS)),
            dma((CHUNKS, CHIPS)),
            dma((CHUNKS,)),
            dma((CHUNKS,)),
        ],
        compiler_params=pltpu.CompilerParams(
            collective_id=0, has_side_effects=True, vmem_limit_bytes=44 * 1024 * 1024
        ),
    )(
        queries, key_weight, value_weight, enc_gain.reshape(1, -1), neighbour_states, slot_dest.reshape(1, -1),
    )


def solution(mesh):
    in_specs = (
        P("phase", "seq", "mp"),
        P("phase", None, "mp"),
        P("phase", None, "mp"),
        P(),
        P("seq", ("phase", "mp"), None),
        P("seq"),
    )
    out_specs = P("phase", "seq", "mp")
    return jax.shard_map(
        on_device, mesh=mesh, in_specs=in_specs, out_specs=out_specs, check_vma=False
    )
```

```python
import jax
import jax.numpy as jnp
from jax import lax
from jax.experimental import pallas as pl
from jax.experimental.pallas import tpu as pltpu
from jax.sharding import PartitionSpec as P

MESH = pl.DeviceIdType.MESH
BF = jnp.bfloat16
F32 = jnp.float32

HD = 128
SEGLEN = 64
SEQ = 16
CHIPS = 8
CHUNKS = 4
ORDER = (1, 0, 2, 3)
EXP2_SCALE = HD ** (-0.5) * 1.4426950408889634


def iota(shape, dim):
    return lax.broadcasted_iota(jnp.int32, shape, dim)


def pack_rows(states_ref, gain_ref, dest_ref, sbuf, mbuf):
    states = states_ref[...].astype(F32)
    meansq = jnp.mean(states * states, axis=-1, keepdims=True)
    normed = states * lax.rsqrt(meansq + 1e-06) * gain_ref[...].reshape(1, 1, -1)
    dest = dest_ref[...]
    row = iota((128, 32), 0)
    hit = lax.shift_right_arithmetic(dest, 4) == row // 8
    before = (iota((32, 32), 0) < iota((32, 32), 1)).astype(BF)
    rank = jnp.dot(hit.astype(BF), before, preferred_element_type=F32)
    pick = hit & (rank == ((row // 4) % 2).astype(F32))
    packed = jnp.zeros((128, 1024), F32)
    for r in range(4):
        one = (pick & (row % 4 == r)).astype(BF)
        packed += jnp.dot(one, normed[:, r, :].astype(BF), preferred_element_type=F32)
    left = packed[:, :512].reshape(SEQ, 8, 512)
    right = packed[:, 512:].reshape(SEQ, 8, 512)
    sbuf[...] = jnp.concatenate([left, right], axis=1).astype(BF)
    hit = lax.shift_right_arithmetic(dest, 4) == iota((SEQ, 32), 0)
    rank = jnp.dot(hit.astype(BF), before, preferred_element_type=F32)
    first, second = [
        jnp.sum(jnp.where(hit & (rank == k), dest + 1, 0), axis=1, keepdims=True) for k in (0.0, 1.0)
    ]
    lane = iota((SEQ, 128), 1)
    place = jnp.where(lane == 0, first, jnp.where(lane == 1, second, 0))
    for d in range(SEQ):
        mbuf[d] = place[d : d + 1]


def unpack_rows(rbuf, mrec, me, piece):
    row, lane = iota((128, 128), 0), iota((128, 128), 1)
    source = (iota((128, SEQ), 0) // 8 == iota((128, SEQ), 1)).astype(BF)
    place = jnp.dot(source, mrec[:, 0, :].astype(F32).astype(BF), preferred_element_type=F32)
    place = jnp.sum(jnp.where(lane == (row // 4) % 2, place, 0.0), axis=1, keepdims=True)
    got = rbuf[...].astype(F32)
    want = SEQ * me + 2 * (lane // 8 - 1) + (lane // 4) % 2 + 1
    match = (place == want.astype(F32)) & (row % 4 == lane % 4) & (lane >= 8) & (lane < 72)
    match = match.astype(BF)
    for half in range(2):
        rows = got[:, 8 * half : 8 * half + 8].reshape(128, 512).astype(BF)
        out = lax.dot_general(match, rows, (((0,), (0,)), ((), ())), preferred_element_type=F32)
        piece[:, 512 * half : 512 * half + 512] = out[:80].astype(BF)


def by_window(rows):
    four = rows.reshape(16, 2, 8, rows.shape[1])
    return [four[:, w].reshape(128, rows.shape[1]).astype(BF) for w in range(2)]


def attend(c, gath, wk, wv, qs, outs):
    near = gath[c].reshape(256, 1024)
    last = iota((16, 256), 0) == 15
    zero = jnp.zeros((SEGLEN, HD), BF)
    pad = jnp.zeros((128, 128), BF)
    pairs = range(8)
    at = [pl.multiple_of(SEGLEN * (2 * c + w), SEGLEN) for w in range(2)]
    cols = [pl.ds(256 * n, 256) for n in pairs]

    def project(weight, n):
        return jnp.concatenate(by_window(jnp.dot(near, weight[:, cols[n]], preferred_element_type=F32)), axis=0)

    def score(n, key):
        left = []
        for w in range(2):
            head = qs[pl.ds(at[w] + 16, 48), cols[n]]
            tail = jnp.where(last, qs[pl.ds(at[w], 16), cols[n]], qs[pl.ds(at[w] + 64, 16), cols[n]])
            query = jnp.concatenate([head, tail], axis=0)
            left.append(jnp.concatenate([query[:, :HD], zero], axis=1))
            left.append(jnp.concatenate([zero, query[:, HD:]], axis=1))
        return lax.dot_general(
            jnp.concatenate(left, axis=0), key, (((1,), (1,)), ((), ())), preferred_element_type=F32
        )

    def finish(n, scores, val):
        weights = []
        for w in range(2):
            own = scores[128 * w : 128 * w + 128, 128 * w : 128 * w + 128]
            top = jnp.max(own, axis=-1, keepdims=True)
            exponent = jnp.exp2((own - top) * EXP2_SCALE)
            total = jnp.sum(exponent, axis=-1, keepdims=True)
            own = (exponent * (1.0 / total)).astype(BF)
            weights.append(jnp.concatenate([own, pad] if w == 0 else [pad, own], axis=1))
        context = jnp.dot(jnp.concatenate(weights, axis=0), val, preferred_element_type=F32)
        for w in range(2):
            two = context[128 * w : 128 * w + 128]
            both = jnp.concatenate([two[:SEGLEN, :HD], two[SEGLEN:, HD:]], axis=1)
            both = both.astype(BF)
            outs[pl.ds(at[w] + 16, 48), cols[n]] = both[:48]
            outs[pl.ds(at[w], 16), cols[n]] = jnp.where(last, both[48:], outs[pl.ds(at[w], 16), cols[n]])
            outs[pl.ds(at[w] + 64, 16), cols[n]] = jnp.where(last, outs[pl.ds(at[w] + 64, 16), cols[n]], both[48:])

    keys = [project(wk, n) for n in pairs]
    scores = [score(n, keys[n]) for n in pairs]
    vals = [project(wv, n) for n in pairs]
    for n in pairs:
        finish(n, scores[n], vals[n])


def kernel(
    q_hbm, wk_hbm, wv_hbm, gain_ref, states_ref, dest_ref, out_hbm,
    sbuf, rbuf, mbuf, mrec, piece, prev, gath, wk, wv, qs, outs, back,
    load_sem, route_send, route_recv, meta_send, meta_recv, halo_send, halo_recv, gath_send, gath_recv, pair_send, pair_recv,
):
    phase, me, mp = lax.axis_index("phase"), lax.axis_index("seq"), lax.axis_index("mp")
    x, core = phase // 2, phase % 2
    chip = x * 2 + mp

    def at_seq(s):
        return (phase, s, mp)

    def at_chip(k):
        return ((k // 2) * 2 + core, me, k % 2)

    after, ahead = lax.rem(me + 1, SEQ), lax.rem(me + SEQ - 1, SEQ)
    partner = (x * 2 + 1 - core, me, mp)
    barrier = pltpu.get_barrier_semaphore()
    for off in range(1, SEQ):
        pl.semaphore_signal(barrier, inc=1, device_id=at_seq(lax.rem(me + off, SEQ)), device_id_type=MESH)
    for off in range(1, CHIPS):
        pl.semaphore_signal(barrier, inc=1, device_id=at_chip(lax.rem(chip + off, CHIPS)), device_id_type=MESH)
    pl.semaphore_signal(barrier, inc=1, device_id=partner, device_id_type=MESH)

    loads = [
        pltpu.make_async_copy(q_hbm.at[0], qs.at[pl.ds(16, 512)], load_sem.at[0]),
        pltpu.make_async_copy(wk_hbm.at[0], wk, load_sem.at[1]),
        pltpu.make_async_copy(wv_hbm.at[0], wv, load_sem.at[2]),
    ]
    for load in loads:
        load.start()
    pack_rows(states_ref, gain_ref, dest_ref, sbuf, mbuf)
    outs[0:16] = jnp.zeros((16, 2048), BF)
    pl.semaphore_wait(barrier, SEQ - 1 + CHIPS - 1 + 1)

    def route(s, slot):
        return pltpu.make_async_remote_copy(
            src_ref=sbuf.at[s], dst_ref=rbuf.at[slot], send_sem=route_send.at[s], recv_sem=route_recv.at[slot],
            device_id=at_seq(s), device_id_type=MESH,
        )

    def inform(s, slot):
        return pltpu.make_async_remote_copy(
            src_ref=mbuf.at[s], dst_ref=mrec.at[slot], send_sem=meta_send.at[s], recv_sem=meta_recv.at[slot],
            device_id=at_seq(s), device_id_type=MESH,
        )

    for off in range(1, SEQ):
        inform(lax.rem(me + off, SEQ), me).start()
        route(lax.rem(me + off, SEQ), me).start()
    query_halo = pltpu.make_async_remote_copy(
        src_ref=q_hbm.at[0, pl.ds(496, 16)], dst_ref=qs.at[pl.ds(0, 16)],
        send_sem=halo_send.at[0], recv_sem=halo_recv.at[0], device_id=at_seq(after), device_id_type=MESH,
    )
    query_halo.start()
    rbuf[me] = sbuf[me]
    mrec[me] = mbuf[me]
    for off in range(1, SEQ):
        s = lax.rem(me + SEQ - off, SEQ)
        inform(s, s).wait_recv()
        route(s, s).wait_recv()
    unpack_rows(rbuf, mrec, me, piece)

    prev_halo = pltpu.make_async_remote_copy(
        src_ref=piece.at[pl.ds(64, 16)], dst_ref=prev,
        send_sem=halo_send.at[1], recv_sem=halo_recv.at[1], device_id=at_seq(after), device_id_type=MESH,
    )
    prev_halo.start()

    def give(c, k, slot):
        return pltpu.make_async_remote_copy(
            src_ref=gath.at[c, core, chip], dst_ref=gath.at[c, core, slot],
            send_sem=gath_send.at[c, k], recv_sem=gath_recv.at[c, slot],
            device_id=at_chip(k), device_id_type=MESH,
        )

    def across(c, side):
        return pltpu.make_async_remote_copy(
            src_ref=gath.at[c, core], dst_ref=gath.at[c, side], send_sem=pair_send.at[c], recv_sem=pair_recv.at[c],
            device_id=partner, device_id_type=MESH,
        )

    for c in ORDER:
        if c == 0:
            prev_halo.wait_recv()
            mine = jnp.where(iota((16, 1024), 0) < 8, prev[...], piece[0:16])
        else:
            mine = piece[16 * c : 16 * c + 16]
        gath[c, core, chip] = mine
        for off in range(1, CHIPS):
            give(c, lax.rem(chip + off, CHIPS), chip).start()

    def pass_on(c):
        for off in range(1, CHIPS):
            k = lax.rem(chip + CHIPS - off, CHIPS)
            give(c, k, k).wait_recv()
        across(c, core).start()

    ctx_halo = pltpu.make_async_remote_copy(
        src_ref=outs.at[pl.ds(0, 16)], dst_ref=back,
        send_sem=halo_send.at[2], recv_sem=halo_recv.at[2], device_id=at_seq(ahead), device_id_type=MESH,
    )
    pass_on(ORDER[0])
    for load in loads:
        load.wait()
    query_halo.wait_recv()

    def step(i, carry):
        c = jnp.where(i < 2, 1 - i, i)
        across(c, 1 - core).wait_recv()

        @pl.when(i + 1 < CHUNKS)
        def _():
            pass_on(jnp.where(i < 1, 0, i + 1))

        attend(c, gath, wk, wv, qs, outs)

        @pl.when(c == 0)
        def _():
            ctx_halo.start()

        return carry

    lax.fori_loop(0, CHUNKS, step, 0)
    ctx_halo.wait_recv()
    outs[512:528] = jnp.where(iota((16, 2048), 0) == 15, back[...], outs[512:528])
    store = pltpu.make_async_copy(outs.at[pl.ds(16, 512)], out_hbm.at[0], load_sem.at[3])
    store.start()
    for off in range(1, SEQ):
        inform(lax.rem(me + off, SEQ), me).wait_send()
        route(lax.rem(me + off, SEQ), me).wait_send()
    query_halo.wait_send()
    prev_halo.wait_send()
    ctx_halo.wait_send()
    for c in ORDER:
        for off in range(1, CHIPS):
            give(c, lax.rem(chip + off, CHIPS), chip).wait_send()
        across(c, core).wait_send()
    store.wait()


def on_device(queries, key_weight, value_weight, enc_gain, neighbour_states, slot_dest):
    place = pl.BlockSpec(memory_space=pl.ANY)
    whole = pl.BlockSpec(memory_space=pltpu.VMEM)
    dma = pltpu.SemaphoreType.DMA
    context = pl.pallas_call(
        kernel,
        out_shape=jax.ShapeDtypeStruct(queries.shape, BF),
        in_specs=[place, place, place, whole, whole, whole],
        out_specs=place,
        scratch_shapes=[
            pltpu.VMEM((SEQ, 16, 512), BF),
            pltpu.VMEM((SEQ, 16, 512), BF),
            pltpu.VMEM((SEQ, 1, 128), jnp.int32),
            pltpu.VMEM((SEQ, 1, 128), jnp.int32),
            pltpu.VMEM((80, 1024), BF),
            pltpu.VMEM((16, 1024), BF),
            pltpu.VMEM((CHUNKS, 2, CHIPS, 16, 1024), BF),
            pltpu.VMEM((1024, 2048), BF),
            pltpu.VMEM((1024, 2048), BF),
            pltpu.VMEM((528, 2048), BF),
            pltpu.VMEM((528, 2048), BF),
            pltpu.VMEM((16, 2048), BF),
            dma((4,)),
            dma((SEQ,)),
            dma((SEQ,)),
            dma((SEQ,)),
            dma((SEQ,)),
            dma((3,)),
            dma((3,)),
            dma((CHUNKS, CHIPS)),
            dma((CHUNKS, CHIPS)),
            dma((CHUNKS,)),
            dma((CHUNKS,)),
        ],
        compiler_params=pltpu.CompilerParams(
            collective_id=0, has_side_effects=True, vmem_limit_bytes=51 * 1024 * 1024
        ),
    )(
        queries, key_weight, value_weight, enc_gain.reshape(1, -1), neighbour_states, slot_dest.reshape(1, -1),
    )
    silent = (iota(context.shape, 1) < SEGLEN - 1) & (lax.axis_index("seq") == 0)
    return jnp.where(silent, jnp.zeros_like(context), context)


def solution(mesh):
    in_specs = (
        P("phase", "seq", "mp"),
        P("phase", None, "mp"),
        P("phase", None, "mp"),
        P(),
        P("seq", ("phase", "mp"), None),
        P("seq"),
    )
    out_specs = P("phase", "seq", "mp")
    return jax.shard_map(
        on_device, mesh=mesh, in_specs=in_specs, out_specs=out_specs, check_vma=False
    )
```

```python
import jax
import jax.numpy as jnp
from jax import lax
from jax.experimental import pallas as pl
from jax.experimental.pallas import tpu as pltpu
from jax.sharding import PartitionSpec as P

MESH = pl.DeviceIdType.MESH
BF = jnp.bfloat16
F32 = jnp.float32

HD = 128
SEGLEN = 64
SEQ = 16
CHIPS = 8
CHUNKS = 4
ORDER = (1, 2, 0, 3)
EXP2_SCALE = HD ** (-0.5) * 1.4426950408889634


def iota(shape, dim):
    return lax.broadcasted_iota(jnp.int32, shape, dim)


def pack_rows(states_ref, gain_ref, dest_ref, sbuf, mbuf):
    states = states_ref[...].astype(F32)
    meansq = jnp.mean(states * states, axis=-1, keepdims=True)
    normed = states * lax.rsqrt(meansq + 1e-06) * gain_ref[...].reshape(1, 1, -1)
    dest = dest_ref[...]
    row = iota((128, 32), 0)
    hit = lax.shift_right_arithmetic(dest, 4) == row // 8
    before = (iota((32, 32), 0) < iota((32, 32), 1)).astype(BF)
    rank = jnp.dot(hit.astype(BF), before, preferred_element_type=F32)
    pick = hit & (rank == ((row // 4) % 2).astype(F32))
    packed = jnp.zeros((128, 1024), F32)
    for r in range(4):
        one = (pick & (row % 4 == r)).astype(BF)
        packed += jnp.dot(one, normed[:, r, :].astype(BF), preferred_element_type=F32)
    left = packed[:, :512].reshape(SEQ, 8, 512)
    right = packed[:, 512:].reshape(SEQ, 8, 512)
    sbuf[...] = jnp.concatenate([left, right], axis=1).astype(BF)
    hit = lax.shift_right_arithmetic(dest, 4) == iota((SEQ, 32), 0)
    rank = jnp.dot(hit.astype(BF), before, preferred_element_type=F32)
    first, second = [
        jnp.sum(jnp.where(hit & (rank == k), dest + 1, 0), axis=1, keepdims=True) for k in (0.0, 1.0)
    ]
    lane = iota((SEQ, 128), 1)
    place = jnp.where(lane == 0, first, jnp.where(lane == 1, second, 0))
    for d in range(SEQ):
        mbuf[d] = place[d : d + 1]


def unpack_rows(rbuf, mrec, me, piece):
    row, lane = iota((128, 128), 0), iota((128, 128), 1)
    source = (iota((128, SEQ), 0) // 8 == iota((128, SEQ), 1)).astype(BF)
    place = jnp.dot(source, mrec[:, 0, :].astype(F32).astype(BF), preferred_element_type=F32)
    place = jnp.sum(jnp.where(lane == (row // 4) % 2, place, 0.0), axis=1, keepdims=True)
    got = rbuf[...].astype(F32)
    want = SEQ * me + 2 * (lane // 8 - 1) + (lane // 4) % 2 + 1
    match = (place == want.astype(F32)) & (row % 4 == lane % 4) & (lane >= 8) & (lane < 72)
    match = match.astype(BF)
    for half in range(2):
        rows = got[:, 8 * half : 8 * half + 8].reshape(128, 512).astype(BF)
        out = lax.dot_general(match, rows, (((0,), (0,)), ((), ())), preferred_element_type=F32)
        piece[:, 512 * half : 512 * half + 512] = out[:80].astype(BF)


def by_window(rows):
    four = rows.reshape(16, 2, 8, rows.shape[1])
    return [four[:, w].reshape(128, rows.shape[1]).astype(BF) for w in range(2)]


def attend(c, gath, wk, wv, qs, outs, tails):
    near = gath[c].reshape(256, 1024)
    last = iota((16, 256), 0) == 15
    zero = jnp.zeros((SEGLEN, HD), BF)
    pad = jnp.zeros((128, 128), BF)
    pairs = range(8)
    at = [pl.multiple_of(SEGLEN * (2 * c + w), SEGLEN) for w in range(2)]
    cols = [pl.ds(256 * n, 256) for n in pairs]

    def project(weight, n):
        return jnp.concatenate(by_window(jnp.dot(near, weight[:, cols[n]], preferred_element_type=F32)), axis=0)

    def score(n, key):
        left = []
        for w in range(2):
            head = qs[pl.ds(at[w] + 16, 48), cols[n]]
            tail = jnp.where(last, qs[pl.ds(at[w], 16), cols[n]], qs[pl.ds(at[w] + 64, 16), cols[n]])
            query = jnp.concatenate([head, tail], axis=0)
            left.append(jnp.concatenate([query[:, :HD], zero], axis=1))
            left.append(jnp.concatenate([zero, query[:, HD:]], axis=1))
        return lax.dot_general(
            jnp.concatenate(left, axis=0), key, (((1,), (1,)), ((), ())), preferred_element_type=F32
        )

    def finish(n, scores, val):
        weights = []
        for w in range(2):
            own = scores[128 * w : 128 * w + 128, 128 * w : 128 * w + 128]
            top = jnp.max(own, axis=-1, keepdims=True)
            exponent = jnp.exp2((own - top) * EXP2_SCALE)
            total = jnp.sum(exponent, axis=-1, keepdims=True)
            own = (exponent * (1.0 / total)).astype(BF)
            weights.append(jnp.concatenate([own, pad] if w == 0 else [pad, own], axis=1))
        context = jnp.dot(jnp.concatenate(weights, axis=0), val, preferred_element_type=F32)
        for w in range(2):
            two = context[128 * w : 128 * w + 128]
            both = jnp.concatenate([two[:SEGLEN, :HD], two[SEGLEN:, HD:]], axis=1)
            both = both.astype(BF)
            outs[pl.ds(at[w], 48), cols[n]] = both[:48]
            tail = pl.ds(at[w] + 48, 16)
            outs[tail, cols[n]] = jnp.where(last, outs[tail, cols[n]], both[48:])
            if w == 0:
                tails[c, :, cols[n]] = both[48:]
            else:
                tail = pl.ds(at[w] - 16, 16)
                outs[tail, cols[n]] = jnp.where(last, both[48:], outs[tail, cols[n]])

    keys = [project(wk, n) for n in pairs]
    scores = [score(n, keys[n]) for n in pairs]
    vals = [project(wv, n) for n in pairs]
    for n in pairs:
        finish(n, scores[n], vals[n])


def kernel(
    q_hbm, wk_hbm, wv_hbm, gain_ref, states_ref, dest_ref, outs,
    sbuf, rbuf, mbuf, mrec, piece, prev, gath, wk, wv, qs, tails, slim, back,
    load_sem, route_send, route_recv, meta_send, meta_recv, halo_send, halo_recv, gath_send, gath_recv, pair_send, pair_recv,
):
    phase, me, mp = lax.axis_index("phase"), lax.axis_index("seq"), lax.axis_index("mp")
    x, core = phase // 2, phase % 2
    chip = x * 2 + mp

    def at_seq(s):
        return (phase, s, mp)

    def at_chip(k):
        return ((k // 2) * 2 + core, me, k % 2)

    after, ahead = lax.rem(me + 1, SEQ), lax.rem(me + SEQ - 1, SEQ)
    partner = (x * 2 + 1 - core, me, mp)
    barrier = pltpu.get_barrier_semaphore()
    for off in range(1, SEQ):
        pl.semaphore_signal(barrier, inc=1, device_id=at_seq(lax.rem(me + off, SEQ)), device_id_type=MESH)
    for off in range(1, CHIPS):
        pl.semaphore_signal(barrier, inc=1, device_id=at_chip(lax.rem(chip + off, CHIPS)), device_id_type=MESH)
    pl.semaphore_signal(barrier, inc=1, device_id=partner, device_id_type=MESH)

    loads = [
        pltpu.make_async_copy(q_hbm.at[0], qs.at[pl.ds(16, 512)], load_sem.at[0]),
        pltpu.make_async_copy(wk_hbm.at[0], wk, load_sem.at[1]),
        pltpu.make_async_copy(wv_hbm.at[0], wv, load_sem.at[2]),
    ]
    for load in loads:
        load.start()
    pack_rows(states_ref, gain_ref, dest_ref, sbuf, mbuf)
    pl.semaphore_wait(barrier, SEQ - 1 + CHIPS - 1 + 1)

    def route(s, slot):
        return pltpu.make_async_remote_copy(
            src_ref=sbuf.at[s], dst_ref=rbuf.at[slot], send_sem=route_send.at[s], recv_sem=route_recv.at[slot],
            device_id=at_seq(s), device_id_type=MESH,
        )

    def inform(s, slot):
        return pltpu.make_async_remote_copy(
            src_ref=mbuf.at[s], dst_ref=mrec.at[slot], send_sem=meta_send.at[s], recv_sem=meta_recv.at[slot],
            device_id=at_seq(s), device_id_type=MESH,
        )

    for off in range(1, SEQ):
        inform(lax.rem(me + off, SEQ), me).start()
        route(lax.rem(me + off, SEQ), me).start()
    query_halo = pltpu.make_async_remote_copy(
        src_ref=q_hbm.at[0, pl.ds(496, 16)], dst_ref=qs.at[pl.ds(0, 16)],
        send_sem=halo_send.at[0], recv_sem=halo_recv.at[0], device_id=at_seq(after), device_id_type=MESH,
    )
    query_halo.start()
    rbuf[me] = sbuf[me]
    mrec[me] = mbuf[me]
    for off in range(1, SEQ):
        s = lax.rem(me + SEQ - off, SEQ)
        inform(s, s).wait_recv()
        route(s, s).wait_recv()
    unpack_rows(rbuf, mrec, me, piece)

    prev_halo = pltpu.make_async_remote_copy(
        src_ref=piece.at[pl.ds(64, 16)], dst_ref=prev,
        send_sem=halo_send.at[1], recv_sem=halo_recv.at[1], device_id=at_seq(after), device_id_type=MESH,
    )
    prev_halo.start()

    def give(c, k, slot):
        return pltpu.make_async_remote_copy(
            src_ref=gath.at[c, core, chip], dst_ref=gath.at[c, core, slot],
            send_sem=gath_send.at[c, k], recv_sem=gath_recv.at[c, slot],
            device_id=at_chip(k), device_id_type=MESH,
        )

    def across(c, side):
        return pltpu.make_async_remote_copy(
            src_ref=gath.at[c, core], dst_ref=gath.at[c, side], send_sem=pair_send.at[c], recv_sem=pair_recv.at[c],
            device_id=partner, device_id_type=MESH,
        )

    def send_own(c):
        @pl.when(c == 0)
        def _():
            prev_halo.wait_recv()

        mine = piece[pl.ds(pl.multiple_of(16 * c, 16), 16), :]
        gath[c, core, chip] = jnp.where((iota((16, 1024), 0) < 8) & (c == 0), prev[...], mine)
        for off in range(1, CHIPS):
            give(c, lax.rem(chip + off, CHIPS), chip).start()

    def sent(c):
        for off in range(1, CHIPS):
            give(c, lax.rem(chip + off, CHIPS), chip).wait_send()

    def pass_on(c):
        for off in range(1, CHIPS):
            k = lax.rem(chip + CHIPS - off, CHIPS)
            give(c, k, k).wait_recv()
        across(c, core).start()

    ctx_halo = pltpu.make_async_remote_copy(
        src_ref=slim, dst_ref=back,
        send_sem=halo_send.at[2], recv_sem=halo_recv.at[2], device_id=at_seq(ahead), device_id_type=MESH,
    )
    send_own(jnp.int32(ORDER[0]))
    send_own(jnp.int32(ORDER[1]))
    pass_on(ORDER[0])
    send_own(jnp.int32(ORDER[2]))
    send_own(jnp.int32(ORDER[3]))
    for load in loads:
        load.wait()
    query_halo.wait_recv()

    def nth(i):
        return sum(jnp.where(i == j, c, 0) for j, c in enumerate(ORDER))

    def step(i, carry):
        c = nth(i)

        @pl.when(i + 1 < CHUNKS)
        def _():
            pass_on(nth(i + 1))

        across(c, 1 - core).wait_recv()
        attend(c, gath, wk, wv, qs, outs, tails)

        @pl.when(c == 0)
        def _():
            rows = jnp.zeros((16, HD), F32)
            for h in range(16):
                row = tails[0, :, HD * h : HD * h + HD].astype(F32)[15:16]
                rows = jnp.where(iota((16, HD), 0) == h, jnp.broadcast_to(row, (16, HD)), rows)
            slim[...] = rows.astype(BF)
            ctx_halo.start()

        @pl.when(c > 0)
        def _():
            tail = pl.ds(pl.multiple_of(2 * SEGLEN * c - 16, 16), 16)
            outs[tail, :] = jnp.where(iota((16, 2048), 0) == 15, tails[c], outs[tail, :])

        return carry

    lax.fori_loop(0, CHUNKS, step, 0)
    ctx_halo.wait_recv()
    back_rows = back[...].astype(F32)
    for h in range(16):
        col = slice(HD * h, HD * h + HD)
        row = jnp.broadcast_to(back_rows[h : h + 1], (16, HD)).astype(BF)
        outs[496:512, col] = jnp.where(iota((16, HD), 0) == 15, row, outs[496:512, col])
    for off in range(1, SEQ):
        inform(lax.rem(me + off, SEQ), me).wait_send()
        route(lax.rem(me + off, SEQ), me).wait_send()
    query_halo.wait_send()
    prev_halo.wait_send()
    ctx_halo.wait_send()
    sent(ORDER[0])
    sent(ORDER[1])
    sent(ORDER[2])
    sent(ORDER[3])
    for c in ORDER:
        across(c, core).wait_send()


def on_device(queries, key_weight, value_weight, enc_gain, neighbour_states, slot_dest):
    place = pl.BlockSpec(memory_space=pl.ANY)
    whole = pl.BlockSpec(memory_space=pltpu.VMEM)
    dma = pltpu.SemaphoreType.DMA
    context = pl.pallas_call(
        kernel,
        out_shape=jax.ShapeDtypeStruct((512, 2048), BF),
        in_specs=[place, place, place, whole, whole, whole],
        out_specs=whole,
        scratch_shapes=[
            pltpu.VMEM((SEQ, 16, 512), BF),
            pltpu.VMEM((SEQ, 16, 512), BF),
            pltpu.VMEM((SEQ, 1, 128), jnp.int32),
            pltpu.VMEM((SEQ, 1, 128), jnp.int32),
            pltpu.VMEM((80, 1024), BF),
            pltpu.VMEM((16, 1024), BF),
            pltpu.VMEM((CHUNKS, 2, CHIPS, 16, 1024), BF),
            pltpu.VMEM((1024, 2048), BF),
            pltpu.VMEM((1024, 2048), BF),
            pltpu.VMEM((528, 2048), BF),
            pltpu.VMEM((CHUNKS, 16, 2048), BF),
            pltpu.VMEM((16, HD), BF),
            pltpu.VMEM((16, HD), BF),
            dma((3,)),
            dma((SEQ,)),
            dma((SEQ,)),
            dma((SEQ,)),
            dma((SEQ,)),
            dma((3,)),
            dma((3,)),
            dma((CHUNKS, CHIPS)),
            dma((CHUNKS, CHIPS)),
            dma((CHUNKS,)),
            dma((CHUNKS,)),
        ],
        compiler_params=pltpu.CompilerParams(
            collective_id=0, has_side_effects=True, vmem_limit_bytes=52000 * 1024
        ),
    )(
        queries, key_weight, value_weight, enc_gain.reshape(1, -1), neighbour_states, slot_dest.reshape(1, -1),
    )
    context = context[None]
    silent = (iota(context.shape, 1) < SEGLEN - 1) & (lax.axis_index("seq") == 0)
    return jnp.where(silent, jnp.zeros_like(context), context)


def solution(mesh):
    in_specs = (
        P("phase", "seq", "mp"),
        P("phase", None, "mp"),
        P("phase", None, "mp"),
        P(),
        P("seq", ("phase", "mp"), None),
        P("seq"),
    )
    out_specs = P("phase", "seq", "mp")
    return jax.shard_map(
        on_device, mesh=mesh, in_specs=in_specs, out_specs=out_specs, check_vma=False
    )
```

```python
import jax
import jax.numpy as jnp
from jax import lax
from jax.experimental import pallas as pl
from jax.experimental.pallas import tpu as pltpu
from jax.sharding import PartitionSpec as P

MESH = pl.DeviceIdType.MESH
BF = jnp.bfloat16
F32 = jnp.float32

HD = 128
SEGLEN = 64
SEQ = 16
CHIPS = 8
CHUNKS = 4
ORDER = (1, 2, 0, 3)
EXP2_SCALE = HD ** (-0.5) * 1.4426950408889634


def iota(shape, dim):
    return lax.broadcasted_iota(jnp.int32, shape, dim)


def pack_rows(states_ref, gain_ref, dest_ref, sbuf, mbuf):
    states = states_ref[...].astype(F32)
    meansq = jnp.mean(states * states, axis=-1, keepdims=True)
    normed = states * lax.rsqrt(meansq + 1e-06) * gain_ref[...].reshape(1, 1, -1)
    dest = dest_ref[...]
    row = iota((128, 32), 0)
    hit = lax.shift_right_arithmetic(dest, 4) == row // 8
    before = (iota((32, 32), 0) < iota((32, 32), 1)).astype(BF)
    rank = jnp.dot(hit.astype(BF), before, preferred_element_type=F32)
    pick = hit & (rank == ((row // 4) % 2).astype(F32))
    packed = jnp.zeros((128, 1024), F32)
    for r in range(4):
        one = (pick & (row % 4 == r)).astype(BF)
        packed += jnp.dot(one, normed[:, r, :].astype(BF), preferred_element_type=F32)
    left = packed[:, :512].reshape(SEQ, 8, 512)
    right = packed[:, 512:].reshape(SEQ, 8, 512)
    sbuf[...] = jnp.concatenate([left, right], axis=1).astype(BF)
    hit = lax.shift_right_arithmetic(dest, 4) == iota((SEQ, 32), 0)
    rank = jnp.dot(hit.astype(BF), before, preferred_element_type=F32)
    first, second = [
        jnp.sum(jnp.where(hit & (rank == k), dest + 1, 0), axis=1, keepdims=True) for k in (0.0, 1.0)
    ]
    lane = iota((SEQ, 128), 1)
    place = jnp.where(lane == 0, first, jnp.where(lane == 1, second, 0))
    for d in range(SEQ):
        mbuf[d] = place[d : d + 1]


def unpack_rows(rbuf, mrec, me, piece):
    row, lane = iota((128, 128), 0), iota((128, 128), 1)
    source = (iota((128, SEQ), 0) // 8 == iota((128, SEQ), 1)).astype(BF)
    place = jnp.dot(source, mrec[:, 0, :].astype(F32).astype(BF), preferred_element_type=F32)
    place = jnp.sum(jnp.where(lane == (row // 4) % 2, place, 0.0), axis=1, keepdims=True)
    got = rbuf[...].astype(F32)
    want = SEQ * me + 2 * (lane // 8 - 1) + (lane // 4) % 2 + 1
    match = (place == want.astype(F32)) & (row % 4 == lane % 4) & (lane >= 8) & (lane < 72)
    match = match.astype(BF)
    for half in range(2):
        rows = got[:, 8 * half : 8 * half + 8].reshape(128, 512).astype(BF)
        out = lax.dot_general(match, rows, (((0,), (0,)), ((), ())), preferred_element_type=F32)
        piece[:, 512 * half : 512 * half + 512] = out[:80].astype(BF)


def by_window(rows):
    four = rows.reshape(16, 2, 8, rows.shape[1])
    return [four[:, w].reshape(128, rows.shape[1]).astype(BF) for w in range(2)]


def attend(c, gath, wk, wv, qs, outs, tails):
    near = gath[c].reshape(256, 1024)
    last = iota((16, 256), 0) == 15
    zero = jnp.zeros((SEGLEN, HD), BF)
    pad = jnp.zeros((128, 128), BF)
    pairs = range(8)
    at = [pl.multiple_of(SEGLEN * (2 * c + w), SEGLEN) for w in range(2)]
    cols = [pl.ds(256 * n, 256) for n in pairs]

    def project(weight, n):
        return jnp.concatenate(by_window(jnp.dot(near, weight[:, cols[n]], preferred_element_type=F32)), axis=0)

    def score(n, key):
        left = []
        for w in range(2):
            head = qs[pl.ds(at[w] + 16, 48), cols[n]]
            tail = jnp.where(last, qs[pl.ds(at[w], 16), cols[n]], qs[pl.ds(at[w] + 64, 16), cols[n]])
            query = jnp.concatenate([head, tail], axis=0)
            left.append(jnp.concatenate([query[:, :HD], zero], axis=1))
            left.append(jnp.concatenate([zero, query[:, HD:]], axis=1))
        return lax.dot_general(
            jnp.concatenate(left, axis=0), key, (((1,), (1,)), ((), ())), preferred_element_type=F32
        )

    def finish(n, scores, val):
        weights = []
        for w in range(2):
            own = scores[128 * w : 128 * w + 128, 128 * w : 128 * w + 128]
            top = jnp.max(own, axis=-1, keepdims=True)
            exponent = jnp.exp2((own - top) * EXP2_SCALE)
            total = jnp.sum(exponent, axis=-1, keepdims=True)
            own = (exponent * (1.0 / total)).astype(BF)
            weights.append(jnp.concatenate([own, pad] if w == 0 else [pad, own], axis=1))
        context = jnp.dot(jnp.concatenate(weights, axis=0), val, preferred_element_type=F32)
        for w in range(2):
            two = context[128 * w : 128 * w + 128]
            both = jnp.concatenate([two[:SEGLEN, :HD], two[SEGLEN:, HD:]], axis=1)
            both = both.astype(BF)
            outs[pl.ds(at[w], 48), cols[n]] = both[:48]
            tail = pl.ds(at[w] + 48, 16)
            outs[tail, cols[n]] = jnp.where(last, outs[tail, cols[n]], both[48:])
            if w == 0:
                tails[c, :, cols[n]] = both[48:]
            else:
                tail = pl.ds(at[w] - 16, 16)
                outs[tail, cols[n]] = jnp.where(last, both[48:], outs[tail, cols[n]])

    keys = [project(wk, n) for n in pairs]
    scores = [score(n, keys[n]) for n in pairs]
    vals = [project(wv, n) for n in pairs]
    for n in pairs:
        finish(n, scores[n], vals[n])


def last_row_by_head(tile):
    rows = jnp.zeros((16, HD), F32)
    for h in range(16):
        row = tile[:, HD * h : HD * h + HD].astype(F32)[15:16]
        rows = jnp.where(iota((16, HD), 0) == h, jnp.broadcast_to(row, (16, HD)), rows)
    return rows.astype(BF)


def kernel(
    q_hbm, wk_hbm, wv_hbm, gain_ref, states_ref, dest_ref, outs,
    sbuf, rbuf, mbuf, mrec, piece, prev, gath, wk, wv, qs, edge, tails, slim, back,
    load_sem, route_send, route_recv, meta_send, meta_recv, halo_send, halo_recv, gath_send, gath_recv, pair_send, pair_recv,
):
    phase, me, mp = lax.axis_index("phase"), lax.axis_index("seq"), lax.axis_index("mp")
    x, core = phase // 2, phase % 2
    chip = x * 2 + mp

    def at_seq(s):
        return (phase, s, mp)

    def at_chip(k):
        return ((k // 2) * 2 + core, me, k % 2)

    after, ahead = lax.rem(me + 1, SEQ), lax.rem(me + SEQ - 1, SEQ)
    partner = (x * 2 + 1 - core, me, mp)
    barrier = pltpu.get_barrier_semaphore()
    for off in range(1, SEQ):
        pl.semaphore_signal(barrier, inc=1, device_id=at_seq(lax.rem(me + off, SEQ)), device_id_type=MESH)
    for off in range(1, CHIPS):
        pl.semaphore_signal(barrier, inc=1, device_id=at_chip(lax.rem(chip + off, CHIPS)), device_id_type=MESH)
    pl.semaphore_signal(barrier, inc=1, device_id=partner, device_id_type=MESH)

    edge_load = pltpu.make_async_copy(q_hbm.at[0, pl.ds(496, 16)], edge, load_sem.at[3])
    edge_load.start()
    loads = [
        pltpu.make_async_copy(q_hbm.at[0], qs.at[pl.ds(16, 512)], load_sem.at[0]),
        pltpu.make_async_copy(wk_hbm.at[0], wk, load_sem.at[1]),
        pltpu.make_async_copy(wv_hbm.at[0], wv, load_sem.at[2]),
    ]
    for load in loads:
        load.start()
    pack_rows(states_ref, gain_ref, dest_ref, sbuf, mbuf)
    edge_load.wait()
    slim[0] = last_row_by_head(edge[...])
    pl.semaphore_wait(barrier, SEQ - 1 + CHIPS - 1 + 1)

    def route(s, slot):
        return pltpu.make_async_remote_copy(
            src_ref=sbuf.at[s], dst_ref=rbuf.at[slot], send_sem=route_send.at[s], recv_sem=route_recv.at[slot],
            device_id=at_seq(s), device_id_type=MESH,
        )

    def inform(s, slot):
        return pltpu.make_async_remote_copy(
            src_ref=mbuf.at[s], dst_ref=mrec.at[slot], send_sem=meta_send.at[s], recv_sem=meta_recv.at[slot],
            device_id=at_seq(s), device_id_type=MESH,
        )

    for off in range(1, SEQ):
        inform(lax.rem(me + off, SEQ), me).start()
        route(lax.rem(me + off, SEQ), me).start()
    query_halo = pltpu.make_async_remote_copy(
        src_ref=slim.at[0], dst_ref=back.at[0],
        send_sem=halo_send.at[0], recv_sem=halo_recv.at[0], device_id=at_seq(after), device_id_type=MESH,
    )
    query_halo.start()
    rbuf[me] = sbuf[me]
    mrec[me] = mbuf[me]
    for off in range(1, SEQ):
        s = lax.rem(me + SEQ - off, SEQ)
        inform(s, s).wait_recv()
        route(s, s).wait_recv()
    unpack_rows(rbuf, mrec, me, piece)

    prev_halo = pltpu.make_async_remote_copy(
        src_ref=piece.at[pl.ds(64, 16)], dst_ref=prev,
        send_sem=halo_send.at[1], recv_sem=halo_recv.at[1], device_id=at_seq(after), device_id_type=MESH,
    )
    prev_halo.start()

    def give(c, k, slot):
        return pltpu.make_async_remote_copy(
            src_ref=gath.at[c, core, chip], dst_ref=gath.at[c, core, slot],
            send_sem=gath_send.at[c, k], recv_sem=gath_recv.at[c, slot],
            device_id=at_chip(k), device_id_type=MESH,
        )

    def across(c, side):
        return pltpu.make_async_remote_copy(
            src_ref=gath.at[c, core], dst_ref=gath.at[c, side], send_sem=pair_send.at[c], recv_sem=pair_recv.at[c],
            device_id=partner, device_id_type=MESH,
        )

    def send_own(c):
        @pl.when(c == 0)
        def _():
            prev_halo.wait_recv()

        mine = piece[pl.ds(pl.multiple_of(16 * c, 16), 16), :]
        gath[c, core, chip] = jnp.where((iota((16, 1024), 0) < 8) & (c == 0), prev[...], mine)
        for off in range(1, CHIPS):
            give(c, lax.rem(chip + off, CHIPS), chip).start()

    def sent(c):
        for off in range(1, CHIPS):
            give(c, lax.rem(chip + off, CHIPS), chip).wait_send()

    def pass_on(c):
        for off in range(1, CHIPS):
            k = lax.rem(chip + CHIPS - off, CHIPS)
            give(c, k, k).wait_recv()
        across(c, core).start()

    ctx_halo = pltpu.make_async_remote_copy(
        src_ref=slim.at[1], dst_ref=back.at[1],
        send_sem=halo_send.at[2], recv_sem=halo_recv.at[2], device_id=at_seq(ahead), device_id_type=MESH,
    )
    send_own(jnp.int32(ORDER[0]))
    send_own(jnp.int32(ORDER[1]))
    pass_on(ORDER[0])
    send_own(jnp.int32(ORDER[2]))
    send_own(jnp.int32(ORDER[3]))
    for load in loads:
        load.wait()
    query_halo.wait_recv()
    query_rows = back[0].astype(F32)
    for h in range(16):
        row = jnp.broadcast_to(query_rows[h : h + 1], (16, HD))
        qs[0:16, HD * h : HD * h + HD] = row.astype(BF)

    def nth(i):
        return sum(jnp.where(i == j, c, 0) for j, c in enumerate(ORDER))

    def step(i, carry):
        c = nth(i)

        @pl.when(i + 1 < CHUNKS)
        def _():
            pass_on(nth(i + 1))

        across(c, 1 - core).wait_recv()
        attend(c, gath, wk, wv, qs, outs, tails)

        @pl.when(c == 0)
        def _():
            slim[1] = last_row_by_head(tails[0])
            ctx_halo.start()

        @pl.when(c > 0)
        def _():
            tail = pl.ds(pl.multiple_of(2 * SEGLEN * c - 16, 16), 16)
            outs[tail, :] = jnp.where(iota((16, 2048), 0) == 15, tails[c], outs[tail, :])

        return carry

    lax.fori_loop(0, CHUNKS, step, 0)
    ctx_halo.wait_recv()
    back_rows = back[1].astype(F32)
    for h in range(16):
        col = slice(HD * h, HD * h + HD)
        row = jnp.broadcast_to(back_rows[h : h + 1], (16, HD)).astype(BF)
        outs[496:512, col] = jnp.where(iota((16, HD), 0) == 15, row, outs[496:512, col])
    for off in range(1, SEQ):
        inform(lax.rem(me + off, SEQ), me).wait_send()
        route(lax.rem(me + off, SEQ), me).wait_send()
    query_halo.wait_send()
    prev_halo.wait_send()
    ctx_halo.wait_send()
    sent(ORDER[0])
    sent(ORDER[1])
    sent(ORDER[2])
    sent(ORDER[3])
    for c in ORDER:
        across(c, core).wait_send()


def on_device(queries, key_weight, value_weight, enc_gain, neighbour_states, slot_dest):
    place = pl.BlockSpec(memory_space=pl.ANY)
    whole = pl.BlockSpec(memory_space=pltpu.VMEM)
    dma = pltpu.SemaphoreType.DMA
    context = pl.pallas_call(
        kernel,
        out_shape=jax.ShapeDtypeStruct((512, 2048), BF),
        in_specs=[place, place, place, whole, whole, whole],
        out_specs=whole,
        scratch_shapes=[
            pltpu.VMEM((SEQ, 16, 512), BF),
            pltpu.VMEM((SEQ, 16, 512), BF),
            pltpu.VMEM((SEQ, 1, 128), jnp.int32),
            pltpu.VMEM((SEQ, 1, 128), jnp.int32),
            pltpu.VMEM((80, 1024), BF),
            pltpu.VMEM((16, 1024), BF),
            pltpu.VMEM((CHUNKS, 2, CHIPS, 16, 1024), BF),
            pltpu.VMEM((1024, 2048), BF),
            pltpu.VMEM((1024, 2048), BF),
            pltpu.VMEM((528, 2048), BF),
            pltpu.VMEM((16, 2048), BF),
            pltpu.VMEM((CHUNKS, 16, 2048), BF),
            pltpu.VMEM((2, 16, HD), BF),
            pltpu.VMEM((2, 16, HD), BF),
            dma((4,)),
            dma((SEQ,)),
            dma((SEQ,)),
            dma((SEQ,)),
            dma((SEQ,)),
            dma((3,)),
            dma((3,)),
            dma((CHUNKS, CHIPS)),
            dma((CHUNKS, CHIPS)),
            dma((CHUNKS,)),
            dma((CHUNKS,)),
        ],
        compiler_params=pltpu.CompilerParams(
            collective_id=0, has_side_effects=True, vmem_limit_bytes=52000 * 1024
        ),
    )(
        queries, key_weight, value_weight, enc_gain.reshape(1, -1), neighbour_states, slot_dest.reshape(1, -1),
    )
    context = context[None]
    silent = (iota(context.shape, 1) < SEGLEN - 1) & (lax.axis_index("seq") == 0)
    return jnp.where(silent, jnp.zeros_like(context), context)


def solution(mesh):
    in_specs = (
        P("phase", "seq", "mp"),
        P("phase", None, "mp"),
        P("phase", None, "mp"),
        P(),
        P("seq", ("phase", "mp"), None),
        P("seq"),
    )
    out_specs = P("phase", "seq", "mp")
    return jax.shard_map(
        on_device, mesh=mesh, in_specs=in_specs, out_specs=out_specs, check_vma=False
    )
```

```python
import jax
import jax.numpy as jnp
from jax import lax
from jax.experimental import pallas as pl
from jax.experimental.pallas import tpu as pltpu
from jax.sharding import PartitionSpec as P

MESH = pl.DeviceIdType.MESH
BF = jnp.bfloat16
F32 = jnp.float32

HD = 128
SEGLEN = 64
SEQ = 16
CHIPS = 8
CHUNKS = 4
ORDER = (1, 2, 0, 3)
EXP2_SCALE = HD ** (-0.5) * 1.4426950408889634


def iota(shape, dim):
    return lax.broadcasted_iota(jnp.int32, shape, dim)


def pack_rows(states_ref, gain_ref, dest_ref, sbuf, mbuf):
    states = states_ref[...].astype(F32)
    meansq = jnp.mean(states * states, axis=-1, keepdims=True)
    normed = states * lax.rsqrt(meansq + 1e-06) * gain_ref[...].reshape(1, 1, -1)
    dest = dest_ref[...]
    row = iota((128, 32), 0)
    hit = lax.shift_right_arithmetic(dest, 4) == row // 8
    before = (iota((32, 32), 0) < iota((32, 32), 1)).astype(BF)
    rank = jnp.dot(hit.astype(BF), before, preferred_element_type=F32)
    pick = hit & (rank == ((row // 4) % 2).astype(F32))
    packed = jnp.zeros((128, 1024), F32)
    for r in range(4):
        one = (pick & (row % 4 == r)).astype(BF)
        packed += jnp.dot(one, normed[:, r, :].astype(BF), preferred_element_type=F32)
    left = packed[:, :512].reshape(SEQ, 8, 512)
    right = packed[:, 512:].reshape(SEQ, 8, 512)
    sbuf[...] = jnp.concatenate([left, right], axis=1).astype(BF)
    hit = lax.shift_right_arithmetic(dest, 4) == iota((SEQ, 32), 0)
    rank = jnp.dot(hit.astype(BF), before, preferred_element_type=F32)
    first, second = [
        jnp.sum(jnp.where(hit & (rank == k), dest + 1, 0), axis=1, keepdims=True) for k in (0.0, 1.0)
    ]
    lane = iota((SEQ, 128), 1)
    place = jnp.where(lane == 0, first, jnp.where(lane == 1, second, 0))
    for d in range(SEQ):
        mbuf[d] = place[d : d + 1]


def unpack_rows(rbuf, mrec, me, piece):
    row, lane = iota((128, 128), 0), iota((128, 128), 1)
    source = (iota((128, SEQ), 0) // 8 == iota((128, SEQ), 1)).astype(BF)
    place = jnp.dot(source, mrec[:, 0, :].astype(F32).astype(BF), preferred_element_type=F32)
    place = jnp.sum(jnp.where(lane == (row // 4) % 2, place, 0.0), axis=1, keepdims=True)
    got = rbuf[...].astype(F32)
    want = SEQ * me + 2 * (lane // 8 - 1) + (lane // 4) % 2 + 1
    match = (place == want.astype(F32)) & (row % 4 == lane % 4) & (lane >= 8) & (lane < 72)
    match = match.astype(BF)
    for half in range(2):
        rows = got[:, 8 * half : 8 * half + 8].reshape(128, 512).astype(BF)
        out = lax.dot_general(match, rows, (((0,), (0,)), ((), ())), preferred_element_type=F32)
        piece[:, 512 * half : 512 * half + 512] = out[:80].astype(BF)


def by_window(rows):
    four = rows.reshape(16, 2, 8, rows.shape[1])
    return [four[:, w].reshape(128, rows.shape[1]).astype(BF) for w in range(2)]


def attend(c, gath, wk, wv, qs, outs, tails):
    near = gath[c].reshape(256, 1024)
    last = iota((16, 256), 0) == 15
    zero = jnp.zeros((SEGLEN, HD), BF)
    pad = jnp.zeros((128, 128), BF)
    pairs = range(8)
    at = [pl.multiple_of(SEGLEN * (2 * c + w), SEGLEN) for w in range(2)]
    cols = [pl.ds(256 * n, 256) for n in pairs]

    def project(weight, n):
        return jnp.concatenate(by_window(jnp.dot(near, weight[:, cols[n]], preferred_element_type=F32)), axis=0)

    def score(n, key):
        left = []
        for w in range(2):
            head = qs[pl.ds(at[w] + 16, 48), cols[n]]
            tail = jnp.where(last, qs[pl.ds(at[w], 16), cols[n]], qs[pl.ds(at[w] + 64, 16), cols[n]])
            query = jnp.concatenate([head, tail], axis=0)
            left.append(jnp.concatenate([query[:, :HD], zero], axis=1))
            left.append(jnp.concatenate([zero, query[:, HD:]], axis=1))
        return lax.dot_general(
            jnp.concatenate(left, axis=0), key, (((1,), (1,)), ((), ())), preferred_element_type=F32
        )

    def finish(n, scores, val):
        weights = []
        for w in range(2):
            own = scores[128 * w : 128 * w + 128, 128 * w : 128 * w + 128]
            top = jnp.max(own, axis=-1, keepdims=True)
            exponent = jnp.exp2((own - top) * EXP2_SCALE)
            total = jnp.sum(exponent, axis=-1, keepdims=True)
            own = (exponent * (1.0 / total)).astype(BF)
            weights.append(jnp.concatenate([own, pad] if w == 0 else [pad, own], axis=1))
        context = jnp.dot(jnp.concatenate(weights, axis=0), val, preferred_element_type=F32)
        for w in range(2):
            two = context[128 * w : 128 * w + 128]
            both = jnp.concatenate([two[:SEGLEN, :HD], two[SEGLEN:, HD:]], axis=1)
            both = both.astype(BF)
            outs[pl.ds(at[w], 48), cols[n]] = both[:48]
            tail = pl.ds(at[w] + 48, 16)
            outs[tail, cols[n]] = jnp.where(last, outs[tail, cols[n]], both[48:])
            if w == 0:
                tails[c, :, cols[n]] = both[48:]
            else:
                tail = pl.ds(at[w] - 16, 16)
                outs[tail, cols[n]] = jnp.where(last, both[48:], outs[tail, cols[n]])

    keys = [project(wk, n) for n in pairs]
    scores = [score(n, keys[n]) for n in pairs]
    vals = [project(wv, n) for n in pairs]
    for n in pairs:
        finish(n, scores[n], vals[n])


def last_row_by_head(tile):
    rows = jnp.zeros((16, HD), F32)
    for h in range(16):
        row = tile[:, HD * h : HD * h + HD].astype(F32)[15:16]
        rows = jnp.where(iota((16, HD), 0) == h, jnp.broadcast_to(row, (16, HD)), rows)
    return rows.astype(BF)


def kernel(
    q_hbm, wk_hbm, wv_hbm, gain_ref, states_ref, dest_ref, outs,
    sbuf, rbuf, mbuf, mrec, piece, prev, gath, wk, wv, qs, edge, tails, slim, back,
    load_sem, route_send, route_recv, meta_send, meta_recv, halo_send, halo_recv, gath_send, gath_recv, pair_send, pair_recv,
):
    phase, me, mp = lax.axis_index("phase"), lax.axis_index("seq"), lax.axis_index("mp")
    x, core = phase // 2, phase % 2
    chip = x * 2 + mp

    def at_seq(s):
        return (phase, s, mp)

    def at_chip(k):
        return ((k // 2) * 2 + core, me, k % 2)

    after, ahead = lax.rem(me + 1, SEQ), lax.rem(me + SEQ - 1, SEQ)
    partner = (x * 2 + 1 - core, me, mp)
    barrier = pltpu.get_barrier_semaphore()
    for off in range(1, SEQ):
        pl.semaphore_signal(barrier, inc=1, device_id=at_seq(lax.rem(me + off, SEQ)), device_id_type=MESH)
    for off in range(1, CHIPS):
        pl.semaphore_signal(barrier, inc=1, device_id=at_chip(lax.rem(chip + off, CHIPS)), device_id_type=MESH)
    pl.semaphore_signal(barrier, inc=1, device_id=partner, device_id_type=MESH)

    edge_load = pltpu.make_async_copy(q_hbm.at[0, pl.ds(496, 16)], edge, load_sem.at[3])
    edge_load.start()
    loads = [
        pltpu.make_async_copy(q_hbm.at[0], qs.at[pl.ds(16, 512)], load_sem.at[0]),
        pltpu.make_async_copy(wk_hbm.at[0], wk, load_sem.at[1]),
        pltpu.make_async_copy(wv_hbm.at[0], wv, load_sem.at[2]),
    ]
    for load in loads:
        load.start()
    pack_rows(states_ref, gain_ref, dest_ref, sbuf, mbuf)
    edge_load.wait()
    slim[0] = last_row_by_head(edge[...])
    pl.semaphore_wait(barrier, SEQ - 1 + CHIPS - 1 + 1)

    def route(s, slot):
        return pltpu.make_async_remote_copy(
            src_ref=sbuf.at[s], dst_ref=rbuf.at[slot], send_sem=route_send.at[s], recv_sem=route_recv.at[slot],
            device_id=at_seq(s), device_id_type=MESH,
        )

    def inform(s, slot):
        return pltpu.make_async_remote_copy(
            src_ref=mbuf.at[s], dst_ref=mrec.at[slot], send_sem=meta_send.at[s], recv_sem=meta_recv.at[slot],
            device_id=at_seq(s), device_id_type=MESH,
        )

    for off in range(1, SEQ):
        inform(lax.rem(me + off, SEQ), me).start()
        route(lax.rem(me + off, SEQ), me).start()
    query_halo = pltpu.make_async_remote_copy(
        src_ref=slim.at[0], dst_ref=back.at[0],
        send_sem=halo_send.at[0], recv_sem=halo_recv.at[0], device_id=at_seq(after), device_id_type=MESH,
    )
    query_halo.start()
    rbuf[me] = sbuf[me]
    mrec[me] = mbuf[me]
    for off in range(1, SEQ):
        s = lax.rem(me + SEQ - off, SEQ)
        inform(s, s).wait_recv()
        route(s, s).wait_recv()
    unpack_rows(rbuf, mrec, me, piece)

    prev_halo = pltpu.make_async_remote_copy(
        src_ref=piece.at[pl.ds(64, 16)], dst_ref=prev,
        send_sem=halo_send.at[1], recv_sem=halo_recv.at[1], device_id=at_seq(after), device_id_type=MESH,
    )
    prev_halo.start()

    def give(c, k, slot):
        return pltpu.make_async_remote_copy(
            src_ref=gath.at[c, core, chip], dst_ref=gath.at[c, core, slot],
            send_sem=gath_send.at[c, k], recv_sem=gath_recv.at[c, slot],
            device_id=at_chip(k), device_id_type=MESH,
        )

    def across(c, side):
        return pltpu.make_async_remote_copy(
            src_ref=gath.at[c, core], dst_ref=gath.at[c, side], send_sem=pair_send.at[c], recv_sem=pair_recv.at[c],
            device_id=partner, device_id_type=MESH,
        )

    def send_own(c):
        @pl.when(c == 0)
        def _():
            prev_halo.wait_recv()

        mine = piece[pl.ds(pl.multiple_of(16 * c, 16), 16), :]
        gath[c, core, chip] = jnp.where((iota((16, 1024), 0) < 8) & (c == 0), prev[...], mine)
        for off in range(1, CHIPS):
            give(c, lax.rem(chip + off, CHIPS), chip).start()

    def sent(c):
        for off in range(1, CHIPS):
            give(c, lax.rem(chip + off, CHIPS), chip).wait_send()

    def pass_on(c):
        for off in range(1, CHIPS):
            k = lax.rem(chip + CHIPS - off, CHIPS)
            give(c, k, k).wait_recv()
        across(c, core).start()

    ctx_halo = pltpu.make_async_remote_copy(
        src_ref=slim.at[1], dst_ref=back.at[1],
        send_sem=halo_send.at[2], recv_sem=halo_recv.at[2], device_id=at_seq(ahead), device_id_type=MESH,
    )
    send_own(jnp.int32(ORDER[0]))
    send_own(jnp.int32(ORDER[1]))
    pass_on(ORDER[0])
    send_own(jnp.int32(ORDER[2]))
    send_own(jnp.int32(ORDER[3]))
    for load in loads:
        load.wait()
    query_halo.wait_recv()
    query_rows = back[0].astype(F32)
    for h in range(16):
        row = jnp.broadcast_to(query_rows[h : h + 1], (16, HD))
        qs[0:16, HD * h : HD * h + HD] = row.astype(BF)

    def nth(i):
        return sum(jnp.where(i == j, c, 0) for j, c in enumerate(ORDER))

    def step(i, carry):
        c = nth(i)

        @pl.when(i + 1 < CHUNKS)
        def _():
            pass_on(nth(i + 1))

        across(c, 1 - core).wait_recv()
        attend(c, gath, wk, wv, qs, outs, tails)

        @pl.when(c == 0)
        def _():
            slim[1] = last_row_by_head(tails[0])
            ctx_halo.start()

        @pl.when(c > 0)
        def _():
            tail = pl.ds(pl.multiple_of(2 * SEGLEN * c - 16, 16), 16)
            outs[tail, :] = jnp.where(iota((16, 2048), 0) == 15, tails[c], outs[tail, :])

        return carry

    lax.fori_loop(0, CHUNKS, step, 0)
    ctx_halo.wait_recv()
    back_rows = back[1].astype(F32)
    for h in range(16):
        col = slice(HD * h, HD * h + HD)
        row = jnp.broadcast_to(back_rows[h : h + 1], (16, HD)).astype(BF)
        outs[496:512, col] = jnp.where(iota((16, HD), 0) == 15, row, outs[496:512, col])

    @pl.when(me == 0)
    def _():
        outs[0:48, :] = jnp.zeros((48, 2048), BF)
        outs[48:64, :] = jnp.where(iota((16, 2048), 0) == 15, outs[48:64, :], jnp.zeros((16, 2048), BF))

    for off in range(1, SEQ):
        inform(lax.rem(me + off, SEQ), me).wait_send()
        route(lax.rem(me + off, SEQ), me).wait_send()
    query_halo.wait_send()
    prev_halo.wait_send()
    ctx_halo.wait_send()
    sent(ORDER[0])
    sent(ORDER[1])
    sent(ORDER[2])
    sent(ORDER[3])
    for c in ORDER:
        across(c, core).wait_send()


def on_device(queries, key_weight, value_weight, enc_gain, neighbour_states, slot_dest):
    place = pl.BlockSpec(memory_space=pl.ANY)
    whole = pl.BlockSpec(memory_space=pltpu.VMEM)
    dma = pltpu.SemaphoreType.DMA
    context = pl.pallas_call(
        kernel,
        out_shape=jax.ShapeDtypeStruct((512, 2048), BF),
        in_specs=[place, place, place, whole, whole, whole],
        out_specs=whole,
        scratch_shapes=[
            pltpu.VMEM((SEQ, 16, 512), BF),
            pltpu.VMEM((SEQ, 16, 512), BF),
            pltpu.VMEM((SEQ, 1, 128), jnp.int32),
            pltpu.VMEM((SEQ, 1, 128), jnp.int32),
            pltpu.VMEM((80, 1024), BF),
            pltpu.VMEM((16, 1024), BF),
            pltpu.VMEM((CHUNKS, 2, CHIPS, 16, 1024), BF),
            pltpu.VMEM((1024, 2048), BF),
            pltpu.VMEM((1024, 2048), BF),
            pltpu.VMEM((528, 2048), BF),
            pltpu.VMEM((16, 2048), BF),
            pltpu.VMEM((CHUNKS, 16, 2048), BF),
            pltpu.VMEM((2, 16, HD), BF),
            pltpu.VMEM((2, 16, HD), BF),
            dma((4,)),
            dma((SEQ,)),
            dma((SEQ,)),
            dma((SEQ,)),
            dma((SEQ,)),
            dma((3,)),
            dma((3,)),
            dma((CHUNKS, CHIPS)),
            dma((CHUNKS, CHIPS)),
            dma((CHUNKS,)),
            dma((CHUNKS,)),
        ],
        compiler_params=pltpu.CompilerParams(
            collective_id=0, has_side_effects=True, vmem_limit_bytes=52000 * 1024
        ),
    )(
        queries, key_weight, value_weight, enc_gain.reshape(1, -1), neighbour_states, slot_dest.reshape(1, -1),
    )
    context = context[None]
    return context


def solution(mesh):
    in_specs = (
        P("phase", "seq", "mp"),
        P("phase", None, "mp"),
        P("phase", None, "mp"),
        P(),
        P("seq", ("phase", "mp"), None),
        P("seq"),
    )
    out_specs = P("phase", "seq", "mp")
    return jax.shard_map(
        on_device, mesh=mesh, in_specs=in_specs, out_specs=out_specs, check_vma=False
    )
```
